32 devices in a mesh: dp: 4 (over y, core), expert: 4 (over z), etp: 2 (over x).
Axes of the slice: x: 2, y: 2, z: 4, core: 2. Of those that a mesh axis runs over, the one named last changes fastest.
Arguments:
- out_grad: bfloat16 [2048, 3072], P(('dp', 'expert'), 'etp'), may hold values from -6 to 6
- hidden: bfloat16 [2048, 2, 16384], P(('dp', 'expert'), None, 'etp'), may hold values from -0.1796875 to 0.1796875
- gates: bfloat16 [2048, 2], P(('dp', 'expert')), may hold values from 0.049804688 to 1
- expert_ids: int32 [2048, 2], P(('dp', 'expert')), may hold values from 0 to 3, all different within a row; in each aligned block of 128 rows (0 to 127, 128 to 255, ...) at most 80 rows name the same one
- down_weight: bfloat16 [4, 16384, 3072], P('expert', 'etp', 'dp'), may hold values from -0.109375 to 0.109375
Outputs:
- hidden_grad: bfloat16 [2048, 2, 16384], P(('dp', 'expert'), None, 'etp')
- gate_grad: bfloat16 [2048, 2], P(('dp', 'expert'))
- weight_grad: bfloat16 [4, 16384, 3072], P('expert', 'etp', 'dp')
The draws below stay inside these ranges and needn't reach their ends.
Inputs may be any that keep to these rules, and one draw needn't show every extreme that they name: `expert_ids`: the two experts of a token differ. Among the rows of one device no expert is named by more than 80 rows, a bound that some block reaches.
All inputs are finite; a program needn't handle non-finite values.
Results may differ from the reference program's by a relative error of at most 0.0049.
Values may be sent and summed in bfloat16 or wider, within the bound.
No kernel may reach another device: no remote copies, remote signals or barrier semaphores. Data moves between devices by JAX's collectives and lax.ppermute only.
A program may use at most 320 MiB of HBM per device.

```python
import math
import jax
import jax.numpy as jnp
import numpy as np
from jax import lax

D = 3072
FF = 16384
TOP = 2
TOK_DEV = 128
EXPERTS = 4
CAP = 80
TOKENS = 2048
N_DP = 4
N_EXPERT = 4


def block_scale(key, shape, split, low, largest):
    factor_of = 1.0
    for position, blocks in split:
        steps = jax.random.uniform(jax.random.fold_in(jax.random.fold_in(key, 6), position), (blocks,), jnp.float32, low / len(split), largest / len(split))
        factor_of = factor_of * jnp.repeat(jnp.exp(steps), shape[position] // blocks).reshape((-1,) + (1,) * (len(shape) - 1 - position))
    return factor_of


def shared_out(own_key, own, number, rows, count, top, most, slope):
    order = jax.random.permutation(own_key, count)
    crowded, ordinary = load_shares(count, rows * top, most, slope, True), load_shares(count, rows * top, most, slope, False)
    places = jnp.arange(count)

    def named(sizes, offset_by):
        used = int((sizes > 0).sum())
        fixed = max(1, used // 4)
        moved = fixed + (places - fixed + offset_by * (used - fixed)) % max(1, count - fixed)
        return jnp.zeros((count,), jnp.int32).at[order[jnp.where(places < fixed, places, moved)]].set(jnp.asarray(sizes, jnp.int32))

    sizes = jnp.where(number % 4 == 0, named(crowded, number // 4), named(ordinary, number - number // 4 - 1))
    mixed = jax.random.permutation(jax.random.fold_in(own, 3), count)
    giver, receiver = mixed[0:count // 2 * 2:2], mixed[1:count // 2 * 2:2]
    slack = jnp.minimum(sizes[giver] - 1, most - sizes[receiver]) // 2
    slack = jnp.where((giver == order[0]) | (receiver == order[0]) | (sizes[receiver] == 0), 0, jnp.maximum(slack, 0))
    moved = jax.random.randint(jax.random.fold_in(own, 4), (count // 2,), 0, 1 << 20) % (slack + 1)
    sizes = sizes.at[giver].add(-moved).at[receiver].add(moved)
    items = jnp.searchsorted(jnp.cumsum(sizes), jnp.arange(rows * top), side="right").astype(jnp.int32)
    table = items.reshape(top, rows).T
    table = table[jax.random.permutation(jax.random.fold_in(own, 1), rows)]
    offset_by = jax.random.randint(jax.random.fold_in(own, 2), (rows, 1), 0, top)
    return jnp.take_along_axis(table, (jnp.arange(top)[None, :] + offset_by) % top, axis=1)


def load_shares(number_of, total, reach, slope, full):
    weights = [(1 << 20) // math.isqrt(rank ** slope) + 1 for rank in range(1, number_of + 1)]
    largest = reach if full else min(reach, max(-(-total // number_of), total * weights[0] // sum(weights)))
    least = 1 if total - largest >= number_of - 1 else 0
    counts, rest = [largest] + [least] * (number_of - 1), total - largest - least * (number_of - 1)
    while rest > 0:
        candidates = [i for i in range(1, number_of) if counts[i] < largest] or [i for i in range(1, number_of) if counts[i] < reach]
        mass, budget = sum([weights[i] for i in candidates]), rest
        for i in candidates:
            more = min(reach - counts[i], max(1, budget * weights[i] // mass), rest)
            counts[i] = counts[i] + more
            rest = rest - more
    return np.array(counts)


def normal_values(stream_key, extent, width, reach, cuts=(), kind=jnp.bfloat16):
    gain = block_scale(stream_key, extent, cuts, -0.22, 0.18) if cuts else 1.0
    drawn = jax.random.normal(stream_key, extent, jnp.float32) * width * gain
    return jnp.minimum(jnp.maximum(drawn, -reach), reach).astype(kind)


def setup_inputs(seed: int = 0) -> dict:
    key_list = jax.random.split(jax.random.key(seed), 6)
    out_grad = normal_values(key_list[0], (TOKENS, D), 1.0, 6.0, ((0, 16), (1, 2)))
    hidden = normal_values(key_list[1], (TOKENS, TOP, FF), 0.03, 0.1796875, ((0, 16), (2, 2)))
    gates = jnp.clip(jnp.exp(math.log(1.0) - 2.9996462 * jax.random.uniform(key_list[2], (TOKENS, TOP), jnp.float32) ** block_scale(key_list[2], (TOKENS, TOP), ((0, 16),), -0.2, 0.2)), 0.049804688, 1.0).astype(jnp.bfloat16)
    expert_ids_keys = jax.random.split(jax.random.fold_in(key_list[3], 1), TOKENS // TOK_DEV)
    expert_ids_turns = jax.random.permutation(jax.random.fold_in(key_list[3], 3), TOKENS // TOK_DEV)
    expert_ids = jax.vmap(lambda own, number: shared_out(jax.random.fold_in(key_list[3], 2), own, number, TOK_DEV, EXPERTS, TOP, CAP, 2))(expert_ids_keys, expert_ids_turns).reshape((TOKENS, TOP))
    down_weight = normal_values(key_list[4], (EXPERTS, FF, D), D ** -0.5, 0.109375, ((0, 4), (1, 2), (2, 4)))
    return {"out_grad": out_grad, "hidden": hidden, "gates": gates, "expert_ids": expert_ids, "down_weight": down_weight}


def per_expert(expert, weight, out_grad, flat_hidden, flat_gates, flat_ids):
    limit = N_DP * N_EXPERT * CAP
    chosen = flat_ids == expert
    ordering = jnp.argsort(jnp.where(chosen, 0, 1).astype(jnp.int32), stable=True)[:limit].astype(jnp.int32)
    present = chosen[ordering]
    token_rows = (ordering // TOP).astype(jnp.int32)
    row_data = jnp.where(present[:, None], out_grad[token_rows], jnp.zeros((), out_grad.dtype))
    back_proj = lax.dot_general(row_data, weight, (((1,), (1,)), ((), ())), preferred_element_type=jnp.float32)
    gate_here = jnp.where(present, flat_gates[ordering], jnp.zeros((), flat_gates.dtype))
    hidden_here = flat_hidden[ordering].astype(jnp.float32)
    grad_hidden = (gate_here[:, None] * back_proj).astype(jnp.bfloat16)
    grad_gate = jnp.sum(hidden_here * back_proj, axis=1).astype(jnp.bfloat16)
    scaled = (gate_here[:, None] * hidden_here).astype(jnp.bfloat16)
    grad_weight = lax.dot_general(scaled, row_data, (((0,), (0,)), ((), ())), preferred_element_type=jnp.float32).astype(jnp.bfloat16)
    return ordering, present, grad_hidden, grad_gate, grad_weight


def reference(out_grad, hidden, gates, expert_ids, down_weight):
    slots = TOKENS * TOP
    flat_ids = expert_ids.reshape(-1)
    flat_gates = gates.reshape(-1).astype(jnp.float32)
    flat_hidden = hidden.reshape(slots, FF)

    def step(packed):
        expert, weight = packed
        return per_expert(expert, weight, out_grad, flat_hidden, flat_gates, flat_ids)

    ordering, present, grad_hidden, grad_gate, grad_weight = lax.map(step, (jnp.arange(EXPERTS, dtype=jnp.int32), down_weight))
    indices = ordering.reshape(-1)
    live_hidden = jnp.where(present[:, :, None], grad_hidden, jnp.zeros((), grad_hidden.dtype)).reshape(-1, FF)
    live_gate = jnp.where(present, grad_gate, jnp.zeros((), grad_gate.dtype)).reshape(-1)
    hidden_grad = jnp.zeros((slots, FF), grad_hidden.dtype).at[indices].add(live_hidden)
    gate_grad = jnp.zeros((slots,), grad_gate.dtype).at[indices].add(live_gate)
    return hidden_grad.reshape(TOKENS, TOP, FF), gate_grad.reshape(TOKENS, TOP), grad_weight
```

```python
import functools

import jax
import jax.numpy as jnp
from jax import lax
from jax.experimental import pallas as pl
from jax.experimental.pallas import tpu as pltpu
from jax.sharding import PartitionSpec as P

CHUNKS = 4
F32, BF16 = jnp.float32, jnp.bfloat16
NT = (((1,), (1,)), ((), ()))
TN = (((0,), (0,)), ((), ()))


def tile_of(cols, most):
    tile = min(cols, most)
    while cols % tile:
        tile //= 2
    return tile


def params(mib=48):
    return pltpu.CompilerParams(vmem_limit_bytes=mib * 2**20)


SHARE = pl.CostEstimate(flops=30 * 10**9, bytes_accessed=0, transcendentals=0)
TOKEN = jax.ShapeDtypeStruct((8, 128), F32)
TOKEN_SPEC = pl.BlockSpec((8, 128), lambda i: (0, 0))


def place_kernel(place_ref, hidden_ref, *refs):
    rows = jnp.dot(place_ref[...], hidden_ref[...], preferred_element_type=F32)
    refs[-1][...] = rows.astype(BF16)


def place_rows(placing, hidden, after=()):
    slots, rows = placing.shape
    cols = hidden.shape[1]
    tile = tile_of(cols, 2048)
    return pl.pallas_call(
        place_kernel,
        grid=(cols // tile,),
        in_specs=[
            pl.BlockSpec((slots, rows), lambda i: (0, 0)),
            pl.BlockSpec((rows, tile), lambda i: (0, i)),
            *[pl.BlockSpec(memory_space=pl.ANY)] * len(after),
        ],
        out_specs=pl.BlockSpec((slots, tile), lambda i: (0, i)),
        out_shape=jax.ShapeDtypeStruct((slots, cols), BF16),
        compiler_params=params(),
        cost_estimate=SHARE,
        name="place",
    )(placing, hidden, *after)


def part_kernel(row_ref, near_ref, far_ref, *refs):
    here_ref, there_ref = refs[-2:]
    slots = here_ref.shape[0]
    half = near_ref.shape[1]
    total = lax.dot_general(
        row_ref[:, :half], near_ref[...], NT, preferred_element_type=F32
    ) + lax.dot_general(row_ref[:, half:], far_ref[...], NT, preferred_element_type=F32)
    here_ref[...] = total[:slots]
    there_ref[...] = total[slots:].astype(BF16)


def partial_product(rows, near, far, chunk, cols, after=()):
    total, depth = rows.shape
    slots = total // 2
    half = near.shape[1]
    tile = tile_of(cols, 512)
    steps = cols // tile
    weight = pl.BlockSpec((tile, half), lambda i: (chunk * steps + i, 0))
    return pl.pallas_call(
        part_kernel,
        grid=(steps,),
        in_specs=[
            pl.BlockSpec((total, depth), lambda i: (0, 0)),
            weight,
            weight,
            *[pl.BlockSpec(memory_space=pl.ANY)] * len(after),
        ],
        out_specs=[pl.BlockSpec((slots, tile), lambda i: (0, i))] * 2,
        out_shape=[
            jax.ShapeDtypeStruct((slots, cols), F32),
            jax.ShapeDtypeStruct((slots, cols), BF16),
        ],
        compiler_params=params(),
        cost_estimate=SHARE,
        name="partial_product",
    )(rows, near, far, *after)


def sum_kernel(here_ref, other_ref, *refs):
    out_ref, token_ref = refs[-2:]
    out_ref[...] = (here_ref[...] + other_ref[...].astype(F32)).astype(BF16)
    token_ref[...] = jnp.zeros_like(token_ref)


def sum_of_parts(here, other, before, place, count, after=()):
    slots, cols = here.shape
    tile = tile_of(cols, 512)
    steps = cols // tile
    extra = [*after] if before is None else [before, *after]
    return pl.pallas_call(
        sum_kernel,
        grid=(steps,),
        in_specs=[pl.BlockSpec((slots, tile), lambda i: (0, i))] * 2
        + [pl.BlockSpec(memory_space=pl.ANY)] * len(extra),
        out_specs=[
            pl.BlockSpec((slots, tile), lambda i: (0, place * steps + i)),
            TOKEN_SPEC,
        ],
        out_shape=[jax.ShapeDtypeStruct((slots, count * cols), BF16), TOKEN],
        input_output_aliases={} if before is None else {2: 0},
        compiler_params=params(),
        cost_estimate=SHARE,
        name="sum_of_parts",
    )(here, other, *extra)


def copy_kernel(*refs):
    refs[-1][...] = refs[0][...]


def column_chunk(rows, chunk, cols, after=()):
    slots = rows.shape[0]
    tile = tile_of(cols, 1024)
    steps = cols // tile
    return pl.pallas_call(
        copy_kernel,
        grid=(steps,),
        in_specs=[pl.BlockSpec((slots, tile), lambda i: (0, chunk * steps + i))]
        + [pl.BlockSpec(memory_space=pl.ANY)] * len(after),
        out_specs=pl.BlockSpec((slots, tile), lambda i: (0, i)),
        out_shape=jax.ShapeDtypeStruct((slots, cols), BF16),
        compiler_params=params(),
        cost_estimate=SHARE,
        name="column_chunk",
    )(rows, *after)


def weight_kernel(groups, *refs):
    rows_ref, (out_ref, token_ref) = refs[groups], refs[-2:]
    token_ref[...] = jnp.zeros_like(token_ref)
    scaled = jnp.concatenate([r[...] for r in refs[:groups]], axis=0)
    total = lax.dot_general(scaled, rows_ref[...], TN, preferred_element_type=F32)
    out_ref[...] = total.astype(BF16)


def weight_chunk(scaled, row_blocks, before, chunk, cols, units, after=()):
    groups = len(scaled)
    total, width = row_blocks.shape
    slots = total // groups
    tile = tile_of(cols, 512)
    steps = cols // tile
    extra = [*after] if before is None else [before, *after]
    return pl.pallas_call(
        functools.partial(weight_kernel, groups),
        grid=(steps,),
        in_specs=[pl.BlockSpec((slots, tile), lambda i: (0, i))] * groups
        + [pl.BlockSpec((total, width), lambda i: (0, 0))]
        + [pl.BlockSpec(memory_space=pl.ANY)] * len(extra),
        out_specs=[
            pl.BlockSpec((tile, width), lambda i: (chunk * steps + i, 0)),
            TOKEN_SPEC,
        ],
        out_shape=[jax.ShapeDtypeStruct((units, width), BF16), TOKEN],
        input_output_aliases={} if before is None else {groups + 1: 0},
        compiler_params=params(),
        cost_estimate=SHARE,
        name="weight_grad",
    )(*scaled, row_blocks, *extra)


def return_kernel(place_ref, gate_ref, hidden_ref, back_ref, *refs):
    out_ref, part_ref = refs[-2:]
    rows = lax.dot_general(place_ref[...], back_ref[...], TN, preferred_element_type=F32)
    out_ref[...] = (gate_ref[...] * rows).astype(BF16)
    part = jnp.sum(hidden_ref[...].astype(F32) * rows, axis=1, keepdims=True)

    @pl.when(pl.program_id(0) == 0)
    def _():
        part_ref[...] = part

    @pl.when(pl.program_id(0) > 0)
    def _():
        part_ref[...] += part


def return_rows(onehot, gates, hidden, back, before, chunk, after=()):
    slots, rows = onehot.shape
    cols = back.shape[1]
    tile = tile_of(cols, 1024)
    steps = cols // tile
    in_specs = [
        pl.BlockSpec((slots, rows), lambda i: (0, 0)),
        pl.BlockSpec((rows, 1), lambda i: (0, 0)),
        pl.BlockSpec((rows, tile), lambda i: (0, chunk * steps + i)),
        pl.BlockSpec((slots, tile), lambda i: (0, i)),
    ]
    extra = [*after] if before is None else [before, *after]
    return pl.pallas_call(
        return_kernel,
        grid=(steps,),
        in_specs=in_specs + [pl.BlockSpec(memory_space=pl.ANY)] * len(extra),
        out_specs=[
            pl.BlockSpec((rows, tile), lambda i: (0, chunk * steps + i)),
            pl.BlockSpec((rows, 1), lambda i: (0, 0)),
        ],
        out_shape=[
            jax.ShapeDtypeStruct(hidden.shape, BF16),
            jax.ShapeDtypeStruct((rows, 1), F32),
        ],
        input_output_aliases={} if before is None else {4: 0},
        compiler_params=params(),
        cost_estimate=SHARE,
        name="return_rows",
    )(onehot, gates, hidden, back, *extra)


def swap(x, axis, bit):
    n = lax.axis_size(axis)
    return lax.ppermute(x, axis, [(i, i ^ bit) for i in range(n)])


def to_experts(rows):
    return lax.all_to_all(rows, "expert", split_axis=0, concat_axis=0, tiled=True)


def chip_features(rows, width):
    dp = lax.axis_index("dp")
    if lax.axis_size("etp") != 2:
        features = lax.all_gather(rows, "etp", axis=1, tiled=True)

        def part(index):
            return lax.dynamic_slice_in_dim(features, index * width, width, axis=1)

        here = jnp.concatenate([part(dp), part(dp ^ 1)], axis=1)
        there = swap(jnp.concatenate([part(dp ^ 2), part(dp ^ 3)], axis=1), "dp", 2)
        return jnp.concatenate([here, there], axis=0)
    first, second = [], []
    for d in range(4):
        for x in range(2):
            if d // 2 == x:
                first.append((d * 2 + x, d * 2 + 1 - x))
            else:
                first.append((d * 2 + x, (d ^ 2) * 2 + x))
                second.append((d * 2 + x, (d ^ 2) * 2 + 1 - x))
    one = lax.ppermute(rows, ("dp", "etp"), first)
    two = lax.ppermute(rows, ("dp", "etp"), second)
    same = dp // 2 == lax.axis_index("etp")
    here, there = jnp.where(same, rows, one), jnp.where(same, one, two)
    both = jnp.concatenate([here, there], axis=0)
    flipped = jnp.concatenate([both[:, width:], both[:, :width]], axis=1)
    return jnp.where(dp % 2 == 0, both, flipped)


def body(out_grad, hidden, gates, expert_ids, down_weight):
    tokens, choices, ff = hidden.shape
    n = lax.axis_size("expert")
    cap = min(tokens, 5 * tokens // (2 * n))
    slots = n * cap
    cols = ff // CHUNKS
    width = down_weight.shape[2]
    expert = lax.axis_index("expert")

    near_weight = down_weight[0]
    far_weight = swap(near_weight, "dp", 1)

    flat_ids = expert_ids.reshape(-1)
    member = (flat_ids[:, None] == jnp.arange(n, dtype=jnp.int32)[None, :]).astype(jnp.int32)
    earlier = jnp.cumsum(member, axis=0) - member
    target = flat_ids * cap + jnp.sum(earlier * member, axis=1)
    chosen = target[None, :] == jnp.arange(slots, dtype=jnp.int32)[:, None]
    onehot = chosen.astype(BF16)
    flat_gates = gates.reshape(-1)
    float_gates = flat_gates.astype(F32)[:, None]
    placing = jnp.where(chosen, flat_gates[None, :], jnp.zeros((), BF16))
    by_token = jnp.sum(onehot.reshape(slots, tokens, choices), axis=2)

    grad_rows = jnp.dot(by_token, out_grad, preferred_element_type=F32).astype(BF16)
    grad_rows = to_experts(grad_rows)

    flat_hidden = hidden.reshape(tokens * choices, ff)
    sent = place_rows(placing, flat_hidden)
    grad_rows, sent = lax.optimization_barrier((grad_rows, sent))
    scaled = to_experts(sent)
    rows = chip_features(grad_rows, width)

    here, others, near, across, traded = [], [], [], [], []
    hidden_grad, weight_grad = None, None
    gate_parts = []

    def part(j, after):
        h, t = partial_product(rows, near_weight, far_weight, j, cols, after)
        here.append(h)
        others.append(swap(t, "dp", 2))
        return t

    def send(j, after):
        near.append(column_chunk(scaled, j, cols, after))
        across.append(swap(near[j], "dp", 2))
        return near[j]

    def trade(j, after):
        *parts, _ = lax.optimization_barrier((near[j], across[j], after))
        traded.append([swap(p, "dp", 1) for p in parts])

    def weight(j, after):
        parts = [near[j], across[j], *traded[j]]
        return weight_chunk(parts, row_blocks, weight_grad, j, cols, ff, (after,))

    def give_back(back, chunk, after):
        out, part = return_rows(
            onehot, float_gates, flat_hidden, back, hidden_grad, chunk, (after,)
        )
        gate_parts.append(part)
        return out

    token = part(0, ())
    far_rows, _ = lax.optimization_barrier((rows[:, width:], token))
    row_blocks = jnp.concatenate([rows[:, :width], swap(far_rows, "dp", 1)], axis=0)
    token = part(1, (token,))
    token = part(2, (token, others[0]))
    first, token = sum_of_parts(here[0], others[0], None, 0, 2, (token, row_blocks))
    token = part(3, (token, others[1]))
    first, token = sum_of_parts(here[1], others[1], first, 1, 2, (token,))
    second, token = sum_of_parts(here[2], others[2], None, 0, 2, (token,))
    first, _, _ = lax.optimization_barrier((first, token, scaled))
    first_back = to_experts(first)
    token = send(0, (token,))
    second, token = sum_of_parts(here[3], others[3], second, 1, 2, (token,))
    token = send(1, (token,))
    second, _, _ = lax.optimization_barrier((second, first_back, token))
    second_back = to_experts(second)
    token = send(2, (token, across[0], first_back))
    trade(0, token)
    hidden_grad = give_back(first_back, 0, token)
    token = send(3, (gate_parts[0], across[1]))
    trade(1, token)
    weight_grad, token = weight(0, token)
    trade(2, token)
    weight_grad, token = weight(1, token)
    weight_grad, token = weight(2, token)
    hidden_grad = give_back(second_back, 1, token)
    hidden_grad = hidden_grad.reshape(hidden.shape)
    trade(3, hidden_grad)
    weight_grad, _ = weight(3, gate_parts[1])
    gate_total = sum(gate_parts)
    if lax.axis_size("etp") == 2:
        gate_total = gate_total + swap(gate_total, "etp", 1)
    else:
        gate_total = lax.psum(gate_total, "etp")

    return (
        hidden_grad,
        gate_total.astype(BF16).reshape(gates.shape),
        weight_grad[None],
    )


def solution(mesh):
    return jax.shard_map(
        body,
        mesh=mesh,
        in_specs=(
            P(("dp", "expert"), "etp"),
            P(("dp", "expert"), None, "etp"),
            P(("dp", "expert"), None),
            P(("dp", "expert"), None),
            P("expert", "etp", "dp"),
        ),
        out_specs=(
            P(("dp", "expert"), None, "etp"),
            P(("dp", "expert"), None),
            P("expert", "etp", "dp"),
        ),
        check_vma=False,
    )
```

```python
import functools

import jax
import jax.numpy as jnp
from jax import lax
from jax.experimental import pallas as pl
from jax.experimental.pallas import tpu as pltpu
from jax.sharding import PartitionSpec as P

CHUNKS = 4
EARLY = 2
F32, BF16 = jnp.float32, jnp.bfloat16
NT = (((1,), (1,)), ((), ()))
TN = (((0,), (0,)), ((), ()))


def tile_of(cols, most):
    tile = min(cols, most)
    while cols % tile:
        tile //= 2
    return tile


def params(mib=48):
    return pltpu.CompilerParams(vmem_limit_bytes=mib * 2**20)


SHARE = pl.CostEstimate(flops=30 * 10**9, bytes_accessed=0, transcendentals=0)
TOKEN = jax.ShapeDtypeStruct((8, 128), F32)
TOKEN_SPEC = pl.BlockSpec((8, 128), lambda i: (0, 0))


def flat(block):
    return block.reshape(block.shape[0] * block.shape[1], block.shape[2])


def place_kernel(n, last, place_ref, hidden_ref, *out_refs):
    cap = out_refs[0].shape[0]
    rows = jnp.dot(place_ref[...], flat(hidden_ref[...]), preferred_element_type=F32)
    rows = rows.astype(BF16)
    for s in range(n):
        out_refs[s][...] = rows[s * cap : (s + 1) * cap]

    @pl.when(pl.program_id(0) <= last)
    def _():
        out_refs[n][...] = rows[:cap]


def place_rows(placing, hidden, n, own_cols):
    slots, rows = placing.shape
    tokens, choices, cols = hidden.shape
    cap = slots // n
    tile = tile_of(own_cols, tile_of(cols, 1024))
    last = own_cols // tile - 1
    block = pl.BlockSpec((cap, tile), lambda i: (0, i))
    return pl.pallas_call(
        functools.partial(place_kernel, n, last),
        grid=(cols // tile,),
        in_specs=[
            pl.BlockSpec((slots, rows), lambda i: (0, 0)),
            pl.BlockSpec((tokens, choices, tile), lambda i: (0, 0, i)),
        ],
        out_specs=[
            *[block] * n,
            pl.BlockSpec((cap, tile), lambda i: (0, jnp.minimum(i, last))),
        ],
        out_shape=[
            *[jax.ShapeDtypeStruct((cap, cols), BF16)] * n,
            jax.ShapeDtypeStruct((cap, own_cols), BF16),
        ],
        compiler_params=params(),
        cost_estimate=SHARE,
        name="place",
    )(placing, hidden)


def part_kernel(row_ref, near_ref, far_ref, *refs):
    here_ref, there_ref = refs[-2:]
    slots = here_ref.shape[0]
    half = near_ref.shape[1]
    total = lax.dot_general(
        row_ref[:, :half], near_ref[...], NT, preferred_element_type=F32
    ) + lax.dot_general(row_ref[:, half:], far_ref[...], NT, preferred_element_type=F32)
    here_ref[...] = total[:slots]
    there_ref[...] = total[slots:].astype(BF16)


def partial_product(rows, near, far, chunk, cols, after=()):
    total, depth = rows.shape
    slots = total // 2
    half = near.shape[1]
    tile = tile_of(cols, 512)
    steps = cols // tile
    weight = pl.BlockSpec((tile, half), lambda i: (chunk * steps + i, 0))
    return pl.pallas_call(
        part_kernel,
        grid=(steps,),
        in_specs=[
            pl.BlockSpec((total, depth), lambda i: (0, 0)),
            weight,
            weight,
            *[pl.BlockSpec(memory_space=pl.ANY)] * len(after),
        ],
        out_specs=[pl.BlockSpec((slots, tile), lambda i: (0, i))] * 2,
        out_shape=[
            jax.ShapeDtypeStruct((slots, cols), F32),
            jax.ShapeDtypeStruct((slots, cols), BF16),
        ],
        compiler_params=params(),
        cost_estimate=SHARE,
        name="partial_product",
    )(rows, near, far, *after)


def sum_kernel(here_ref, other_ref, *refs):
    out_ref, token_ref = refs[-2:]
    out_ref[...] = (here_ref[...] + other_ref[...].astype(F32)).astype(BF16)
    token_ref[...] = jnp.zeros_like(token_ref)


def sum_of_parts(here, other, before, place, count, after=()):
    slots, cols = here.shape
    tile = tile_of(cols, 512)
    steps = cols // tile
    extra = [*after] if before is None else [before, *after]
    return pl.pallas_call(
        sum_kernel,
        grid=(steps,),
        in_specs=[pl.BlockSpec((slots, tile), lambda i: (0, i))] * 2
        + [pl.BlockSpec(memory_space=pl.ANY)] * len(extra),
        out_specs=[
            pl.BlockSpec((slots, tile), lambda i: (0, place * steps + i)),
            TOKEN_SPEC,
        ],
        out_shape=[jax.ShapeDtypeStruct((slots, count * cols), BF16), TOKEN],
        input_output_aliases={} if before is None else {2: 0},
        compiler_params=params(),
        cost_estimate=SHARE,
        name="sum_of_parts",
    )(here, other, *extra)


def column_chunk(blocks, chunk, cols, after=()):
    count, cap = len(blocks), blocks[0].shape[0]
    tile = tile_of(cols, 1024)
    steps = cols // tile

    def kernel(*refs):
        refs[-1][...] = jnp.concatenate([r[...] for r in refs[:count]], axis=0)

    return pl.pallas_call(
        kernel,
        grid=(steps,),
        in_specs=[pl.BlockSpec((cap, tile), lambda i: (0, chunk * steps + i))] * count
        + [pl.BlockSpec(memory_space=pl.ANY)] * len(after),
        out_specs=pl.BlockSpec((count * cap, tile), lambda i: (0, i)),
        out_shape=jax.ShapeDtypeStruct((count * cap, cols), BF16),
        compiler_params=params(),
        cost_estimate=SHARE,
        name="column_chunk",
    )(*blocks, *after)


def weight_kernel(count, *refs):
    rows_ref, (out_ref, token_ref) = refs[count], refs[-2:]
    token_ref[...] = jnp.zeros_like(token_ref)
    scaled = jnp.concatenate([r[...] for r in refs[:count]], axis=0)
    total = lax.dot_general(scaled, rows_ref[...], TN, preferred_element_type=F32)
    out_ref[...] = total.astype(BF16)


def weight_chunk(scaled, row_blocks, before, chunk, cols, units, after=()):
    count = len(scaled)
    total, width = row_blocks.shape
    tile = tile_of(cols, 512)
    steps = cols // tile
    extra = [*after] if before is None else [before, *after]

    def block(rows):
        start = 0 if rows.shape[1] == cols else chunk * steps
        return pl.BlockSpec((rows.shape[0], tile), lambda i: (0, start + i))

    return pl.pallas_call(
        functools.partial(weight_kernel, count),
        grid=(steps,),
        in_specs=[block(rows) for rows in scaled]
        + [pl.BlockSpec((total, width), lambda i: (0, 0))]
        + [pl.BlockSpec(memory_space=pl.ANY)] * len(extra),
        out_specs=[
            pl.BlockSpec((tile, width), lambda i: (chunk * steps + i, 0)),
            TOKEN_SPEC,
        ],
        out_shape=[jax.ShapeDtypeStruct((units, width), BF16), TOKEN],
        input_output_aliases={} if before is None else {count + 1: 0},
        compiler_params=params(),
        cost_estimate=SHARE,
        name="weight_grad",
    )(*scaled, row_blocks, *extra)


def return_kernel(place_ref, gate_ref, hidden_ref, back_ref, *refs):
    out_ref, part_ref = refs[-2:]
    rows = lax.dot_general(place_ref[...], back_ref[...], TN, preferred_element_type=F32)
    out_ref[...] = (gate_ref[...] * rows).astype(BF16).reshape(out_ref.shape)
    part = jnp.sum(flat(hidden_ref[...]).astype(F32) * rows, axis=1, keepdims=True)

    @pl.when(pl.program_id(0) == 0)
    def _():
        part_ref[...] = part

    @pl.when(pl.program_id(0) > 0)
    def _():
        part_ref[...] += part


def return_rows(onehot, gates, hidden, back, before, start, after=()):
    slots, rows = onehot.shape
    tokens, choices, _ = hidden.shape
    cols = back.shape[1]
    tile = tile_of(cols, 1024)
    steps, first = cols // tile, start // tile
    block = pl.BlockSpec((tokens, choices, tile), lambda i: (0, 0, first + i))
    in_specs = [
        pl.BlockSpec((slots, rows), lambda i: (0, 0)),
        pl.BlockSpec((rows, 1), lambda i: (0, 0)),
        block,
        pl.BlockSpec((slots, tile), lambda i: (0, i)),
    ]
    extra = [*after] if before is None else [before, *after]
    return pl.pallas_call(
        return_kernel,
        grid=(steps,),
        in_specs=in_specs + [pl.BlockSpec(memory_space=pl.ANY)] * len(extra),
        out_specs=[block, pl.BlockSpec((rows, 1), lambda i: (0, 0))],
        out_shape=[
            jax.ShapeDtypeStruct(hidden.shape, BF16),
            jax.ShapeDtypeStruct((rows, 1), F32),
        ],
        input_output_aliases={} if before is None else {4: 0},
        compiler_params=params(),
        cost_estimate=SHARE,
        name="return_rows",
    )(onehot, gates, hidden, back, *extra)


def swap(x, axis, bit):
    n = lax.axis_size(axis)
    return lax.ppermute(x, axis, [(i, i ^ bit) for i in range(n)])


def to_experts(rows):
    return lax.all_to_all(rows, "expert", split_axis=0, concat_axis=0, tiled=True)


def chip_features(rows, width):
    dp = lax.axis_index("dp")
    if lax.axis_size("etp") != 2:
        features = lax.all_gather(rows, "etp", axis=1, tiled=True)

        def part(index):
            return lax.dynamic_slice_in_dim(features, index * width, width, axis=1)

        here = jnp.concatenate([part(dp), part(dp ^ 1)], axis=1)
        there = swap(jnp.concatenate([part(dp ^ 2), part(dp ^ 3)], axis=1), "dp", 2)
        return jnp.concatenate([here, there], axis=0)
    first, second = [], []
    for d in range(4):
        for x in range(2):
            if d // 2 == x:
                first.append((d * 2 + x, d * 2 + 1 - x))
            else:
                first.append((d * 2 + x, (d ^ 2) * 2 + x))
                second.append((d * 2 + x, (d ^ 2) * 2 + 1 - x))
    one = lax.ppermute(rows, ("dp", "etp"), first)
    two = lax.ppermute(rows, ("dp", "etp"), second)
    same = dp // 2 == lax.axis_index("etp")
    here, there = jnp.where(same, rows, one), jnp.where(same, one, two)
    both = jnp.concatenate([here, there], axis=0)
    flipped = jnp.concatenate([both[:, width:], both[:, :width]], axis=1)
    return jnp.where(dp % 2 == 0, both, flipped)


def body(out_grad, hidden, gates, expert_ids, down_weight):
    tokens, choices, ff = hidden.shape
    n = lax.axis_size("expert")
    cap = min(tokens, 5 * tokens // (2 * n))
    slots = n * cap
    cols = ff // CHUNKS
    width = down_weight.shape[2]
    expert = lax.axis_index("expert")

    near_weight = down_weight[0]
    far_weight = swap(near_weight, "dp", 1)

    flat_ids = expert_ids.reshape(-1)
    member = (flat_ids[:, None] == jnp.arange(n, dtype=jnp.int32)[None, :]).astype(jnp.int32)
    earlier = jnp.cumsum(member, axis=0) - member
    target = flat_ids * cap + jnp.sum(earlier * member, axis=1)
    chosen = target[None, :] == jnp.arange(slots, dtype=jnp.int32)[:, None]
    onehot = chosen.astype(BF16)
    flat_gates = gates.reshape(-1)
    float_gates = flat_gates.astype(F32)[:, None]
    moved = ((flat_ids ^ expert) - flat_ids) * cap + target
    chosen = moved[None, :] == jnp.arange(slots, dtype=jnp.int32)[:, None]
    placing = jnp.where(chosen, flat_gates[None, :], jnp.zeros((), BF16))
    by_token = jnp.sum(onehot.reshape(slots, tokens, choices), axis=2)

    grad_rows = jnp.dot(by_token, out_grad, preferred_element_type=F32).astype(BF16)
    grad_rows = to_experts(grad_rows)

    *blocks, own = place_rows(placing, hidden, n, EARLY * cols)
    own_across = swap(own, "dp", 2)
    grad_rows, far_weight, _, *blocks = lax.optimization_barrier(
        (grad_rows, far_weight, own_across, *blocks)
    )
    scaled = [swap(b, "expert", s) if s else b for s, b in enumerate(blocks)]
    rows = chip_features(grad_rows, width)

    here, others, near, across, traded = [], [], [], [], []
    hidden_grad, weight_grad = None, None
    gate_parts = []

    def part(j, after):
        h, t = partial_product(rows, near_weight, far_weight, j, cols, after)
        here.append(h)
        others.append(swap(t, "dp", 2))
        return t

    def send(j, after):
        blocks = scaled[1:] if j < EARLY else scaled
        near.append(column_chunk(blocks, j, cols, after))
        across.append(swap(near[j], "dp", 2))
        return near[j]

    def trade(j, after):
        *parts, _ = lax.optimization_barrier((near[j], across[j], after))
        traded.append([swap(p, "dp", 1) for p in parts])

    def weight(j, after):
        parts = [near[j], across[j], *traded[j]]
        if j < EARLY:
            parts = [p for pair in zip(own_parts, parts) for p in pair]
        return weight_chunk(parts, row_blocks, weight_grad, j, cols, ff, (after,))

    def give_back(back, start, after):
        out, part = return_rows(
            onehot, float_gates, hidden, back, hidden_grad, start, (after,)
        )
        gate_parts.append(part)
        return out

    token = part(0, ())
    token = part(1, (token,))
    token = part(2, (token, others[0]))
    first, token = sum_of_parts(here[0], others[0], None, 0, 2, (token,))
    token = part(3, (token, others[1]))
    first, token = sum_of_parts(here[1], others[1], first, 1, 2, (token,))
    first_back = to_experts(first)
    second, token = sum_of_parts(here[2], others[2], None, 0, 2, (token,))
    token = send(0, (token,))
    far_rows, _ = lax.optimization_barrier((rows[:, width:], token))
    row_blocks = jnp.concatenate([rows[:, :width], swap(far_rows, "dp", 1)], axis=0)
    row_blocks = row_blocks.reshape(4, n, cap, width)
    row_blocks = jnp.concatenate(
        [lax.dynamic_slice_in_dim(row_blocks, expert ^ s, 1, axis=1) for s in range(n)],
        axis=1,
    ).reshape(4 * slots, width)
    second, token = sum_of_parts(here[3], others[3], second, 1, 2, (token,))
    token = send(1, (token, row_blocks))
    *moving, _ = lax.optimization_barrier((own, own_across, token))
    own_parts = [own, own_across, *[swap(p, "dp", 1) for p in moving]]
    token = send(2, (token, across[0]))
    trade(0, token)
    second, _, _ = lax.optimization_barrier((second, first_back, token))
    second_back = to_experts(second)
    hidden_grad = give_back(first_back, 0, token)
    token = send(3, (gate_parts[0], across[1], *own_parts))
    trade(1, token)
    weight_grad, token = weight(0, token)
    trade(2, token)
    weight_grad, token = weight(1, token)
    weight_grad, token = weight(2, token)
    trade(3, token)
    hidden_grad = give_back(second_back, 2 * cols, token)
    weight_grad, token = weight(3, gate_parts[1])
    gate_total = sum(gate_parts)
    if lax.axis_size("etp") == 2:
        other, _ = lax.optimization_barrier((swap(gate_total, "etp", 1), token))
        gate_total = gate_total + other
    else:
        gate_total = lax.psum(gate_total, "etp")

    return (
        hidden_grad,
        gate_total.astype(BF16).reshape(gates.shape),
        weight_grad[None],
    )


def solution(mesh):
    return jax.shard_map(
        body,
        mesh=mesh,
        in_specs=(
            P(("dp", "expert"), "etp"),
            P(("dp", "expert"), None, "etp"),
            P(("dp", "expert"), None),
            P(("dp", "expert"), None),
            P("expert", "etp", "dp"),
        ),
        out_specs=(
            P(("dp", "expert"), None, "etp"),
            P(("dp", "expert"), None),
            P("expert", "etp", "dp"),
        ),
        check_vma=False,
    )
```

```python
import functools
import math

import jax
import jax.numpy as jnp
from jax import lax
from jax.experimental import pallas as pl
from jax.experimental.pallas import tpu as pltpu
from jax.sharding import PartitionSpec as P

SUM_PIECES = (1, 2, 2, 3)
ROW_PIECES = (2, 3, 2, 1)
EARLY = 2
F32, BF16 = jnp.float32, jnp.bfloat16
NT = (((1,), (1,)), ((), ()))
TN = (((0,), (0,)), ((), ()))


def tile_of(cols, most):
    tile = min(cols, most)
    while cols % tile:
        tile //= 2
    return tile


def pieces(eighths, units):
    starts = [sum(eighths[:i]) * units // 8 for i in range(len(eighths) + 1)]
    return [(a, b - a) for a, b in zip(starts, starts[1:])]


def tile_at(start, cols, most):
    return tile_of(math.gcd(start, cols), most)


def params(mib=48):
    return pltpu.CompilerParams(vmem_limit_bytes=mib * 2**20)


def share(micros):
    return pl.CostEstimate(flops=micros * 10**9, bytes_accessed=0, transcendentals=0)


SHARE = share(30)
TOKEN = jax.ShapeDtypeStruct((8, 128), F32)
TOKEN_SPEC = pl.BlockSpec((8, 128), lambda i: (0, 0))


def flat(block):
    return block.reshape(block.shape[0] * block.shape[1], block.shape[2])


def place_kernel(n, place_ref, hidden_ref, *refs):
    out_refs = refs[-n:]
    cap = out_refs[0].shape[0]
    rows = jnp.dot(place_ref[...], flat(hidden_ref[...]), preferred_element_type=F32)
    rows = rows.astype(BF16)
    for s in range(n):
        out_refs[s][...] = rows[s * cap : (s + 1) * cap]


def place_rows(placing, hidden, n, cols, after=()):
    slots, rows = placing.shape
    tokens, choices, _ = hidden.shape
    cap = slots // n
    tile = tile_of(cols, 1024)
    return pl.pallas_call(
        functools.partial(place_kernel, n),
        grid=(cols // tile,),
        in_specs=[
            pl.BlockSpec((slots, rows), lambda i: (0, 0)),
            pl.BlockSpec((tokens, choices, tile), lambda i: (0, 0, i)),
            *[pl.BlockSpec(memory_space=pl.ANY)] * len(after),
        ],
        out_specs=[pl.BlockSpec((cap, tile), lambda i: (0, i))] * n,
        out_shape=[jax.ShapeDtypeStruct((cap, cols), BF16)] * n,
        compiler_params=params(),
        cost_estimate=share(2),
        name="place",
    )(placing, hidden, *after)


def part_kernel(row_ref, near_ref, far_ref, *refs):
    here_ref, there_ref = refs[-2:]
    slots = here_ref.shape[0]
    half = near_ref.shape[1]
    total = lax.dot_general(
        row_ref[:, :half], near_ref[...], NT, preferred_element_type=F32
    ) + lax.dot_general(row_ref[:, half:], far_ref[...], NT, preferred_element_type=F32)
    here_ref[...] = total[:slots]
    there_ref[...] = total[slots:].astype(BF16)


def partial_product(rows, near, far, start, cols, after=()):
    total, depth = rows.shape
    slots = total // 2
    half = near.shape[1]
    tile = tile_at(start, cols, 512)
    steps, first = cols // tile, start // tile
    weight = pl.BlockSpec((tile, half), lambda i: (first + i, 0))
    return pl.pallas_call(
        part_kernel,
        grid=(steps,),
        in_specs=[
            pl.BlockSpec((total, depth), lambda i: (0, 0)),
            weight,
            weight,
            *[pl.BlockSpec(memory_space=pl.ANY)] * len(after),
        ],
        out_specs=[pl.BlockSpec((slots, tile), lambda i: (0, i))] * 2,
        out_shape=[
            jax.ShapeDtypeStruct((slots, cols), F32),
            jax.ShapeDtypeStruct((slots, cols), BF16),
        ],
        compiler_params=params(),
        cost_estimate=SHARE,
        name="partial_product",
    )(rows, near, far, *after)


def sum_kernel(here_ref, other_ref, *refs):
    out_ref, token_ref = refs[-2:]
    out_ref[...] = (here_ref[...] + other_ref[...].astype(F32)).astype(BF16)
    token_ref[...] = jnp.zeros_like(token_ref)


def sum_of_parts(here, other, before, start, total, after=()):
    slots, cols = here.shape
    tile = tile_at(start, cols, 512)
    steps, first = cols // tile, start // tile
    extra = [*after] if before is None else [before, *after]
    return pl.pallas_call(
        sum_kernel,
        grid=(steps,),
        in_specs=[pl.BlockSpec((slots, tile), lambda i: (0, i))] * 2
        + [pl.BlockSpec(memory_space=pl.ANY)] * len(extra),
        out_specs=[
            pl.BlockSpec((slots, tile), lambda i: (0, first + i)),
            TOKEN_SPEC,
        ],
        out_shape=[jax.ShapeDtypeStruct((slots, total), BF16), TOKEN],
        input_output_aliases={} if before is None else {2: 0},
        compiler_params=params(),
        cost_estimate=SHARE,
        name="sum_of_parts",
    )(here, other, *extra)


def column_piece(blocks, start, cols, after=()):
    count, cap = len(blocks), blocks[0].shape[0]
    tile = tile_at(start, cols, 1024)
    steps, first = cols // tile, start // tile

    def kernel(*refs):
        refs[-1][...] = jnp.concatenate([r[...] for r in refs[:count]], axis=0)

    return pl.pallas_call(
        kernel,
        grid=(steps,),
        in_specs=[pl.BlockSpec((cap, tile), lambda i: (0, first + i))] * count
        + [pl.BlockSpec(memory_space=pl.ANY)] * len(after),
        out_specs=pl.BlockSpec((count * cap, tile), lambda i: (0, i)),
        out_shape=jax.ShapeDtypeStruct((count * cap, cols), BF16),
        compiler_params=params(),
        cost_estimate=SHARE,
        name="column_piece",
    )(*blocks, *after)


def weight_kernel(count, *refs):
    rows_ref, (out_ref, token_ref) = refs[count], refs[-2:]
    token_ref[...] = jnp.zeros_like(token_ref)
    scaled = jnp.concatenate([r[...] for r in refs[:count]], axis=0)
    total = lax.dot_general(scaled, rows_ref[...], TN, preferred_element_type=F32)
    out_ref[...] = total.astype(BF16)


def weight_piece(scaled, row_blocks, before, start, cols, units, after=()):
    count = len(scaled)
    total, width = row_blocks.shape
    tile = functools.reduce(math.gcd, [start - at for _, at in scaled], math.gcd(start, cols))
    tile = tile_of(tile, 512)
    steps, first = cols // tile, start // tile
    extra = [*after] if before is None else [before, *after]

    def block(rows, at):
        skip = (start - at) // tile
        return pl.BlockSpec((rows.shape[0], tile), lambda i: (0, skip + i))

    return pl.pallas_call(
        functools.partial(weight_kernel, count),
        grid=(steps,),
        in_specs=[block(*entry) for entry in scaled]
        + [pl.BlockSpec((total, width), lambda i: (0, 0))]
        + [pl.BlockSpec(memory_space=pl.ANY)] * len(extra),
        out_specs=[
            pl.BlockSpec((tile, width), lambda i: (first + i, 0)),
            TOKEN_SPEC,
        ],
        out_shape=[jax.ShapeDtypeStruct((units, width), BF16), TOKEN],
        input_output_aliases={} if before is None else {count + 1: 0},
        compiler_params=params(),
        cost_estimate=SHARE,
        name="weight_grad",
    )(*[rows for rows, _ in scaled], row_blocks, *extra)


def return_kernel(place_ref, gate_ref, hidden_ref, back_ref, *refs):
    out_ref, part_ref = refs[-2:]
    rows = lax.dot_general(place_ref[...], back_ref[...], TN, preferred_element_type=F32)
    out_ref[...] = (gate_ref[...] * rows).astype(BF16).reshape(out_ref.shape)
    part = jnp.sum(flat(hidden_ref[...]).astype(F32) * rows, axis=1, keepdims=True)

    @pl.when(pl.program_id(0) == 0)
    def _():
        part_ref[...] = part

    @pl.when(pl.program_id(0) > 0)
    def _():
        part_ref[...] += part


def return_rows(onehot, gates, hidden, back, before, start, after=()):
    slots, rows = onehot.shape
    tokens, choices, _ = hidden.shape
    cols = back.shape[1]
    tile = tile_at(start, cols, 1024)
    steps, first = cols // tile, start // tile
    block = pl.BlockSpec((tokens, choices, tile), lambda i: (0, 0, first + i))
    in_specs = [
        pl.BlockSpec((slots, rows), lambda i: (0, 0)),
        pl.BlockSpec((rows, 1), lambda i: (0, 0)),
        block,
        pl.BlockSpec((slots, tile), lambda i: (0, i)),
    ]
    extra = [*after] if before is None else [before, *after]
    return pl.pallas_call(
        return_kernel,
        grid=(steps,),
        in_specs=in_specs + [pl.BlockSpec(memory_space=pl.ANY)] * len(extra),
        out_specs=[block, pl.BlockSpec((rows, 1), lambda i: (0, 0))],
        out_shape=[
            jax.ShapeDtypeStruct(hidden.shape, BF16),
            jax.ShapeDtypeStruct((rows, 1), F32),
        ],
        input_output_aliases={} if before is None else {4: 0},
        compiler_params=params(),
        cost_estimate=SHARE,
        name="return_rows",
    )(onehot, gates, hidden, back, *extra)


def swap(x, axis, bit):
    n = lax.axis_size(axis)
    return lax.ppermute(x, axis, [(i, i ^ bit) for i in range(n)])


def to_experts(rows):
    return lax.all_to_all(rows, "expert", split_axis=0, concat_axis=0, tiled=True)


def chip_features(rows, width):
    dp = lax.axis_index("dp")
    if lax.axis_size("etp") != 2:
        features = lax.all_gather(rows, "etp", axis=1, tiled=True)

        def part(index):
            return lax.dynamic_slice_in_dim(features, index * width, width, axis=1)

        here = jnp.concatenate([part(dp), part(dp ^ 1)], axis=1)
        there = swap(jnp.concatenate([part(dp ^ 2), part(dp ^ 3)], axis=1), "dp", 2)
        return jnp.concatenate([here, there], axis=0)
    first, second = [], []
    for d in range(4):
        for x in range(2):
            if d // 2 == x:
                first.append((d * 2 + x, d * 2 + 1 - x))
            else:
                first.append((d * 2 + x, (d ^ 2) * 2 + x))
                second.append((d * 2 + x, (d ^ 2) * 2 + 1 - x))
    one = lax.ppermute(rows, ("dp", "etp"), first)
    two = lax.ppermute(rows, ("dp", "etp"), second)
    same = dp // 2 == lax.axis_index("etp")
    here, there = jnp.where(same, rows, one), jnp.where(same, one, two)
    both = jnp.concatenate([here, there], axis=0)
    flipped = jnp.concatenate([both[:, width:], both[:, :width]], axis=1)
    return jnp.where(dp % 2 == 0, both, flipped)


def body(out_grad, hidden, gates, expert_ids, down_weight):
    tokens, choices, ff = hidden.shape
    n = lax.axis_size("expert")
    cap = min(tokens, 5 * tokens // (2 * n))
    slots = n * cap
    sums, pieces_of_rows = pieces(SUM_PIECES, ff), pieces(ROW_PIECES, ff)
    early = pieces_of_rows[EARLY][0]
    cut = sums[-1][0]
    width = down_weight.shape[2]
    expert = lax.axis_index("expert")

    near_weight = down_weight[0]
    far_weight = swap(near_weight, "dp", 1)

    flat_ids = expert_ids.reshape(-1)
    member = (flat_ids[:, None] == jnp.arange(n, dtype=jnp.int32)[None, :]).astype(jnp.int32)
    earlier = jnp.cumsum(member, axis=0) - member
    target = flat_ids * cap + jnp.sum(earlier * member, axis=1)
    chosen = target[None, :] == jnp.arange(slots, dtype=jnp.int32)[:, None]
    onehot = chosen.astype(BF16)
    flat_gates = gates.reshape(-1)
    float_gates = flat_gates.astype(F32)[:, None]
    moved = ((flat_ids ^ expert) - flat_ids) * cap + target
    chosen = moved[None, :] == jnp.arange(slots, dtype=jnp.int32)[:, None]
    placing = jnp.where(chosen, flat_gates[None, :], jnp.zeros((), BF16))
    by_token = jnp.sum(onehot.reshape(slots, tokens, choices), axis=2)

    grad_rows = jnp.dot(by_token, out_grad, preferred_element_type=F32).astype(BF16)
    grad_rows = to_experts(grad_rows)

    [own] = place_rows(placing[:cap], hidden, 1, early)
    own_across = swap(own, "dp", 2)
    blocks = place_rows(placing, hidden, n, ff, (own,))
    grad_rows, far_weight, _, *blocks = lax.optimization_barrier(
        (grad_rows, far_weight, own_across, *blocks)
    )
    scaled = [swap(b, "expert", s) if s else b for s, b in enumerate(blocks)]
    rows = chip_features(grad_rows, width)

    here, others, near, across, traded = [], [], [], [], []
    hidden_grad, weight_grad = None, None
    gate_parts = []

    def part(j, after):
        h, t = partial_product(rows, near_weight, far_weight, *sums[j], after)
        here.append(h)
        others.append(swap(t, "dp", 2))
        return t

    def send(j, after):
        near.append(column_piece(scaled[1:] if j < EARLY else scaled, *pieces_of_rows[j], after))
        across.append(swap(near[j], "dp", 2))
        return near[j]

    def trade(j, after):
        *parts, _ = lax.optimization_barrier((near[j], across[j], after))
        traded.append([swap(p, "dp", 1) for p in parts])

    def weight(j, after, skip=0, take=8):
        at, cols = pieces_of_rows[j]
        parts = [(p, at) for p in (near[j], across[j], *traded[j])]
        if j < EARLY:
            parts = [p for own, part in zip(own_parts, parts) for p in ((own, 0), part)]
        start = at + skip * ff // 8
        cols = min(cols - skip * ff // 8, take * ff // 8)
        return weight_piece(parts, row_blocks, weight_grad, start, cols, ff, (after,))

    def give_back(back, start, after):
        out, part = return_rows(
            onehot, float_gates, hidden, back, hidden_grad, start, (after,)
        )
        gate_parts.append(part)
        return out

    token = part(0, ())
    token = part(1, (token,))
    token = part(2, (token, others[0]))
    first, token = sum_of_parts(here[0], others[0], None, sums[0][0], cut, (token,))
    token = part(3, (token, others[1]))
    first, token = sum_of_parts(here[1], others[1], first, sums[1][0], cut, (token,))
    first, token = sum_of_parts(here[2], others[2], first, sums[2][0], cut, (token,))
    first_back = to_experts(first)
    token = send(0, (token,))
    far_rows, _ = lax.optimization_barrier((rows[:, width:], token))
    far_rows = swap(far_rows, "dp", 1)
    second, token = sum_of_parts(here[3], others[3], None, 0, ff - cut, (token,))
    far_rows, _ = lax.optimization_barrier((far_rows, token))
    row_blocks = jnp.concatenate([rows[:, :width], far_rows], axis=0)
    row_blocks = row_blocks.reshape(4, n, cap, width)
    row_blocks = jnp.concatenate(
        [lax.dynamic_slice_in_dim(row_blocks, expert ^ s, 1, axis=1) for s in range(n)],
        axis=1,
    ).reshape(4 * slots, width)
    token = send(1, (token, row_blocks))
    *moving, _ = lax.optimization_barrier((own, own_across, token))
    own_parts = [own, own_across, *[swap(p, "dp", 1) for p in moving]]
    token = send(2, (token,))
    trade(0, token)
    token = send(3, (token, *own_parts))
    weight_grad, token = weight(0, token, 0, 1)
    second, _, _ = lax.optimization_barrier((second, first_back, token))
    second_back = to_experts(second)
    hidden_grad = give_back(first_back, 0, token)
    trade(1, gate_parts[0])
    weight_grad, token = weight(0, gate_parts[0], 1)
    weight_grad, token = weight(1, token, 0, 2)
    trade(2, token)
    weight_grad, token = weight(1, token, 2)
    weight_grad, token = weight(2, token)
    trade(3, token)
    hidden_grad = give_back(second_back, cut, token)
    weight_grad, token = weight(3, gate_parts[1])
    gate_total = sum(gate_parts)
    if lax.axis_size("etp") == 2:
        gate_total = gate_total + swap(gate_total, "etp", 1) + token[:1, :1]
    else:
        gate_total = lax.psum(gate_total, "etp")

    return (
        hidden_grad,
        gate_total.astype(BF16).reshape(gates.shape),
        weight_grad[None],
    )


def solution(mesh):
    return jax.shard_map(
        body,
        mesh=mesh,
        in_specs=(
            P(("dp", "expert"), "etp"),
            P(("dp", "expert"), None, "etp"),
            P(("dp", "expert"), None),
            P(("dp", "expert"), None),
            P("expert", "etp", "dp"),
        ),
        out_specs=(
            P(("dp", "expert"), None, "etp"),
            P(("dp", "expert"), None),
            P("expert", "etp", "dp"),
        ),
        check_vma=False,
    )
```

```python
import functools
import math

import jax
import jax.numpy as jnp
from jax import lax
from jax.experimental import pallas as pl
from jax.experimental.pallas import tpu as pltpu
from jax.sharding import PartitionSpec as P

SUM_PIECES = (1, 2, 2, 3)
ROW_PIECES = (2, 3, 1, 1, 1)
EARLY = 2
F32, BF16 = jnp.float32, jnp.bfloat16
NT = (((1,), (1,)), ((), ()))
TN = (((0,), (0,)), ((), ()))


def tile_of(cols, most):
    tile = min(cols, most)
    while cols % tile:
        tile //= 2
    return tile


def pieces(eighths, units):
    starts = [sum(eighths[:i]) * units // 8 for i in range(len(eighths) + 1)]
    return [(a, b - a) for a, b in zip(starts, starts[1:])]


def tile_at(start, cols, most):
    return tile_of(math.gcd(start, cols), most)


def params(mib=48):
    return pltpu.CompilerParams(vmem_limit_bytes=mib * 2**20)


def share(micros):
    return pl.CostEstimate(flops=micros * 10**9, bytes_accessed=0, transcendentals=0)


SHARE = share(30)
TOKEN = jax.ShapeDtypeStruct((8, 128), F32)
TOKEN_SPEC = pl.BlockSpec((8, 128), lambda i: (0, 0))


def flat(block):
    return block.reshape(block.shape[0] * block.shape[1], block.shape[2])


def place_kernel(n, place_ref, hidden_ref, *refs):
    out_refs = refs[-n:]
    cap = out_refs[0].shape[0]
    rows = jnp.dot(place_ref[...], flat(hidden_ref[...]), preferred_element_type=F32)
    rows = rows.astype(BF16)
    for s in range(n):
        out_refs[s][...] = rows[s * cap : (s + 1) * cap]


def place_rows(placing, hidden, n, cols, after=()):
    slots, rows = placing.shape
    tokens, choices, _ = hidden.shape
    cap = slots // n
    tile = tile_of(cols, 1024)
    return pl.pallas_call(
        functools.partial(place_kernel, n),
        grid=(cols // tile,),
        in_specs=[
            pl.BlockSpec((slots, rows), lambda i: (0, 0)),
            pl.BlockSpec((tokens, choices, tile), lambda i: (0, 0, i)),
            *[pl.BlockSpec(memory_space=pl.ANY)] * len(after),
        ],
        out_specs=[pl.BlockSpec((cap, tile), lambda i: (0, i))] * n,
        out_shape=[jax.ShapeDtypeStruct((cap, cols), BF16)] * n,
        compiler_params=params(),
        cost_estimate=share(2),
        name="place",
    )(placing, hidden, *after)


def part_kernel(row_ref, near_ref, far_ref, *refs):
    here_ref, there_ref = refs[-2:]
    slots = here_ref.shape[0]
    half = near_ref.shape[1]
    total = lax.dot_general(
        row_ref[:, :half], near_ref[...], NT, preferred_element_type=F32
    ) + lax.dot_general(row_ref[:, half:], far_ref[...], NT, preferred_element_type=F32)
    here_ref[...] = total[:slots]
    there_ref[...] = total[slots:].astype(BF16)


def partial_product(rows, near, far, start, cols, after=()):
    total, depth = rows.shape
    slots = total // 2
    half = near.shape[1]
    tile = tile_at(start, cols, 512)
    steps, first = cols // tile, start // tile
    weight = pl.BlockSpec((tile, half), lambda i: (first + i, 0))
    return pl.pallas_call(
        part_kernel,
        grid=(steps,),
        in_specs=[
            pl.BlockSpec((total, depth), lambda i: (0, 0)),
            weight,
            weight,
            *[pl.BlockSpec(memory_space=pl.ANY)] * len(after),
        ],
        out_specs=[pl.BlockSpec((slots, tile), lambda i: (0, i))] * 2,
        out_shape=[
            jax.ShapeDtypeStruct((slots, cols), F32),
            jax.ShapeDtypeStruct((slots, cols), BF16),
        ],
        compiler_params=params(),
        cost_estimate=SHARE,
        name="partial_product",
    )(rows, near, far, *after)


def sum_kernel(here_ref, other_ref, *refs):
    out_ref, token_ref = refs[-2:]
    out_ref[...] = (here_ref[...] + other_ref[...].astype(F32)).astype(BF16)
    token_ref[...] = jnp.zeros_like(token_ref)


def sum_of_parts(here, other, before, start, total, after=()):
    slots, cols = here.shape
    tile = tile_at(start, cols, 512)
    steps, first = cols // tile, start // tile
    extra = [*after] if before is None else [before, *after]
    return pl.pallas_call(
        sum_kernel,
        grid=(steps,),
        in_specs=[pl.BlockSpec((slots, tile), lambda i: (0, i))] * 2
        + [pl.BlockSpec(memory_space=pl.ANY)] * len(extra),
        out_specs=[
            pl.BlockSpec((slots, tile), lambda i: (0, first + i)),
            TOKEN_SPEC,
        ],
        out_shape=[jax.ShapeDtypeStruct((slots, total), BF16), TOKEN],
        input_output_aliases={} if before is None else {2: 0},
        compiler_params=params(),
        cost_estimate=SHARE,
        name="sum_of_parts",
    )(here, other, *extra)


def column_piece(blocks, start, cols, after=()):
    count, cap = len(blocks), blocks[0].shape[0]
    tile = tile_at(start, cols, 1024)
    steps, first = cols // tile, start // tile

    def kernel(*refs):
        refs[-1][...] = jnp.concatenate([r[...] for r in refs[:count]], axis=0)

    return pl.pallas_call(
        kernel,
        grid=(steps,),
        in_specs=[pl.BlockSpec((cap, tile), lambda i: (0, first + i))] * count
        + [pl.BlockSpec(memory_space=pl.ANY)] * len(after),
        out_specs=pl.BlockSpec((count * cap, tile), lambda i: (0, i)),
        out_shape=jax.ShapeDtypeStruct((count * cap, cols), BF16),
        compiler_params=params(),
        cost_estimate=SHARE,
        name="column_piece",
    )(*blocks, *after)


def weight_kernel(count, *refs):
    rows_ref, (out_ref, token_ref) = refs[count], refs[-2:]
    token_ref[...] = jnp.zeros_like(token_ref)
    scaled = jnp.concatenate([r[...] for r in refs[:count]], axis=0)
    total = lax.dot_general(scaled, rows_ref[...], TN, preferred_element_type=F32)
    out_ref[...] = total.astype(BF16)


def weight_piece(scaled, row_blocks, before, start, cols, units, after=()):
    count = len(scaled)
    total, width = row_blocks.shape
    tile = functools.reduce(math.gcd, [start - at for _, at in scaled], math.gcd(start, cols))
    tile = tile_of(tile, 512)
    steps, first = cols // tile, start // tile
    extra = [*after] if before is None else [before, *after]

    def block(rows, at):
        skip = (start - at) // tile
        return pl.BlockSpec((rows.shape[0], tile), lambda i: (0, skip + i))

    return pl.pallas_call(
        functools.partial(weight_kernel, count),
        grid=(steps,),
        in_specs=[block(*entry) for entry in scaled]
        + [pl.BlockSpec((total, width), lambda i: (0, 0))]
        + [pl.BlockSpec(memory_space=pl.ANY)] * len(extra),
        out_specs=[
            pl.BlockSpec((tile, width), lambda i: (first + i, 0)),
            TOKEN_SPEC,
        ],
        out_shape=[jax.ShapeDtypeStruct((units, width), BF16), TOKEN],
        input_output_aliases={} if before is None else {count + 1: 0},
        compiler_params=params(),
        cost_estimate=SHARE,
        name="weight_grad",
    )(*[rows for rows, _ in scaled], row_blocks, *extra)


def return_kernel(place_ref, gate_ref, hidden_ref, back_ref, *refs):
    out_ref, part_ref = refs[-2:]
    rows = lax.dot_general(place_ref[...], back_ref[...], TN, preferred_element_type=F32)
    out_ref[...] = (gate_ref[...] * rows).astype(BF16).reshape(out_ref.shape)
    part = jnp.sum(flat(hidden_ref[...]).astype(F32) * rows, axis=1, keepdims=True)

    @pl.when(pl.program_id(0) == 0)
    def _():
        part_ref[...] = part

    @pl.when(pl.program_id(0) > 0)
    def _():
        part_ref[...] += part


def return_rows(onehot, gates, hidden, back, before, start, after=()):
    slots, rows = onehot.shape
    tokens, choices, _ = hidden.shape
    cols = back.shape[1]
    tile = tile_at(start, cols, 1024)
    steps, first = cols // tile, start // tile
    block = pl.BlockSpec((tokens, choices, tile), lambda i: (0, 0, first + i))
    in_specs = [
        pl.BlockSpec((slots, rows), lambda i: (0, 0)),
        pl.BlockSpec((rows, 1), lambda i: (0, 0)),
        block,
        pl.BlockSpec((slots, tile), lambda i: (0, i)),
    ]
    extra = [*after] if before is None else [before, *after]
    return pl.pallas_call(
        return_kernel,
        grid=(steps,),
        in_specs=in_specs + [pl.BlockSpec(memory_space=pl.ANY)] * len(extra),
        out_specs=[block, pl.BlockSpec((rows, 1), lambda i: (0, 0))],
        out_shape=[
            jax.ShapeDtypeStruct(hidden.shape, BF16),
            jax.ShapeDtypeStruct((rows, 1), F32),
        ],
        input_output_aliases={} if before is None else {4: 0},
        compiler_params=params(),
        cost_estimate=SHARE,
        name="return_rows",
    )(onehot, gates, hidden, back, *extra)


def swap(x, axis, bit):
    n = lax.axis_size(axis)
    return lax.ppermute(x, axis, [(i, i ^ bit) for i in range(n)])


def to_experts(rows):
    return lax.all_to_all(rows, "expert", split_axis=0, concat_axis=0, tiled=True)


def chip_features(rows, width):
    dp = lax.axis_index("dp")
    if lax.axis_size("etp") != 2:
        features = lax.all_gather(rows, "etp", axis=1, tiled=True)

        def part(index):
            return lax.dynamic_slice_in_dim(features, index * width, width, axis=1)

        here = jnp.concatenate([part(dp), part(dp ^ 1)], axis=1)
        there = swap(jnp.concatenate([part(dp ^ 2), part(dp ^ 3)], axis=1), "dp", 2)
        return jnp.concatenate([here, there], axis=0)
    first, second = [], []
    for d in range(4):
        for x in range(2):
            if d // 2 == x:
                first.append((d * 2 + x, d * 2 + 1 - x))
            else:
                first.append((d * 2 + x, (d ^ 2) * 2 + x))
                second.append((d * 2 + x, (d ^ 2) * 2 + 1 - x))
    one = lax.ppermute(rows, ("dp", "etp"), first)
    two = lax.ppermute(rows, ("dp", "etp"), second)
    same = dp // 2 == lax.axis_index("etp")
    here, there = jnp.where(same, rows, one), jnp.where(same, one, two)
    both = jnp.concatenate([here, there], axis=0)
    flipped = jnp.concatenate([both[:, width:], both[:, :width]], axis=1)
    return jnp.where(dp % 2 == 0, both, flipped)


def body(out_grad, hidden, gates, expert_ids, down_weight):
    tokens, choices, ff = hidden.shape
    n = lax.axis_size("expert")
    cap = min(tokens, 5 * tokens // (2 * n))
    slots = n * cap
    sums, pieces_of_rows = pieces(SUM_PIECES, ff), pieces(ROW_PIECES, ff)
    early = pieces_of_rows[EARLY][0]
    cut = sums[-1][0]
    width = down_weight.shape[2]
    expert = lax.axis_index("expert")

    near_weight = down_weight[0]
    far_weight = swap(near_weight, "dp", 1)

    flat_ids = expert_ids.reshape(-1)
    member = (flat_ids[:, None] == jnp.arange(n, dtype=jnp.int32)[None, :]).astype(jnp.int32)
    earlier = jnp.cumsum(member, axis=0) - member
    target = flat_ids * cap + jnp.sum(earlier * member, axis=1)
    chosen = target[None, :] == jnp.arange(slots, dtype=jnp.int32)[:, None]
    onehot = chosen.astype(BF16)
    flat_gates = gates.reshape(-1)
    float_gates = flat_gates.astype(F32)[:, None]
    moved = ((flat_ids ^ expert) - flat_ids) * cap + target
    chosen = moved[None, :] == jnp.arange(slots, dtype=jnp.int32)[:, None]
    placing = jnp.where(chosen, flat_gates[None, :], jnp.zeros((), BF16))
    by_token = jnp.sum(chosen.astype(BF16).reshape(slots, tokens, choices), axis=2)

    placed = jnp.dot(by_token, out_grad, preferred_element_type=F32).astype(BF16)
    arrived = [placed[s * cap : (s + 1) * cap] for s in range(n)]
    arrived = [swap(b, "expert", s) if s else b for s, b in enumerate(arrived)]
    grad_rows = jnp.concatenate(arrived, axis=0)
    grad_rows = jnp.concatenate(
        [lax.dynamic_slice_in_dim(grad_rows, (expert ^ e) * cap, cap) for e in range(n)],
        axis=0,
    )

    [own] = place_rows(placing[:cap], hidden, 1, early, (placed,))
    own_across = swap(own, "dp", 2)
    blocks = place_rows(placing, hidden, n, ff, (own,))
    grad_rows, far_weight, _, *blocks = lax.optimization_barrier(
        (grad_rows, far_weight, own_across, *blocks)
    )
    scaled = [swap(b, "expert", s) if s else b for s, b in enumerate(blocks)]
    rows = chip_features(grad_rows, width)

    here, others, near, across, traded = [], [], [], [], []
    hidden_grad, weight_grad = None, None
    gate_parts = []

    def part(j, after):
        h, t = partial_product(rows, near_weight, far_weight, *sums[j], after)
        here.append(h)
        others.append(swap(t, "dp", 2))
        return t

    def send(j, after):
        near.append(column_piece(scaled[1:] if j < EARLY else scaled, *pieces_of_rows[j], after))
        across.append(swap(near[j], "dp", 2))
        return near[j]

    def trade(j, after):
        *parts, _ = lax.optimization_barrier((near[j], across[j], after))
        traded.append([swap(p, "dp", 1) for p in parts])

    def weight(j, after, skip=0, take=16):
        at, cols = pieces_of_rows[j]
        parts = [(p, at) for p in (near[j], across[j], *traded[j])]
        if j < EARLY:
            parts = [p for own, part in zip(own_parts, parts) for p in ((own, 0), part)]
        skip, take = skip * ff // 16, take * ff // 16
        start, cols = at + skip, min(cols - skip, take)
        return weight_piece(parts, row_blocks, weight_grad, start, cols, ff, (after,))

    def give_back(back, start, after):
        out, part = return_rows(
            onehot, float_gates, hidden, back, hidden_grad, start, (after,)
        )
        gate_parts.append(part)
        return out

    token = part(0, ())
    token = part(1, (token,))
    token = part(2, (token, others[0]))
    first, token = sum_of_parts(here[0], others[0], None, sums[0][0], cut, (token,))
    token = part(3, (token, others[1]))
    first, token = sum_of_parts(here[1], others[1], first, sums[1][0], cut, (token,))
    first, token = sum_of_parts(here[2], others[2], first, sums[2][0], cut, (token,))
    first_back = to_experts(first)
    token = send(0, (token,))
    far_rows, _ = lax.optimization_barrier((rows[:, width:], token))
    far_rows = swap(far_rows, "dp", 1)
    second, token = sum_of_parts(here[3], others[3], None, 0, ff - cut, (token,))
    far_rows, _ = lax.optimization_barrier((far_rows, token))
    row_blocks = jnp.concatenate([rows[:, :width], far_rows], axis=0)
    row_blocks = row_blocks.reshape(4, n, cap, width)
    row_blocks = jnp.concatenate(
        [lax.dynamic_slice_in_dim(row_blocks, expert ^ s, 1, axis=1) for s in range(n)],
        axis=1,
    ).reshape(4 * slots, width)
    token = send(1, (token, row_blocks))
    *moving, _ = lax.optimization_barrier((own, own_across, token))
    own_parts = [own, own_across, *[swap(p, "dp", 1) for p in moving]]
    token = send(2, (token,))
    trade(0, token)
    token = send(3, (token, *own_parts))
    weight_grad, token = weight(0, token, 0, 2)
    second, _, _ = lax.optimization_barrier((second, first_back, token))
    second_back = to_experts(second)
    hidden_grad = give_back(first_back, 0, token)
    trade(1, gate_parts[0])
    weight_grad, token = weight(0, gate_parts[0], 2)
    token = send(4, (token,))
    most = 5 if ff % 2048 == 0 else 4
    weight_grad, token = weight(1, token, 0, most)
    trade(2, token)
    weight_grad, token = weight(1, token, most)
    trade(3, token)
    weight_grad, token = weight(2, token)
    weight_grad, token = weight(3, token)
    trade(4, token)
    hidden_grad = give_back(second_back, cut, token)
    weight_grad, token = weight(4, gate_parts[1])
    gate_total = sum(gate_parts)
    if lax.axis_size("etp") == 2:
        gate_total = gate_total + swap(gate_total, "etp", 1) + token[:1, :1]
    else:
        gate_total = lax.psum(gate_total, "etp")

    return (
        hidden_grad,
        gate_total.astype(BF16).reshape(gates.shape),
        weight_grad[None],
    )


def solution(mesh):
    return jax.shard_map(
        body,
        mesh=mesh,
        in_specs=(
            P(("dp", "expert"), "etp"),
            P(("dp", "expert"), None, "etp"),
            P(("dp", "expert"), None),
            P(("dp", "expert"), None),
            P("expert", "etp", "dp"),
        ),
        out_specs=(
            P(("dp", "expert"), None, "etp"),
            P(("dp", "expert"), None),
            P("expert", "etp", "dp"),
        ),
        check_vma=False,
    )
```

```python
import functools
import math

import jax
import jax.numpy as jnp
from jax import lax
from jax.experimental import pallas as pl
from jax.experimental.pallas import tpu as pltpu
from jax.sharding import PartitionSpec as P

SUM_PIECES = (1, 2, 3, 2)
ROW_PIECES = (2, 3, 1, 1, 1)
EARLY = 2
F32, BF16 = jnp.float32, jnp.bfloat16
NT = (((1,), (1,)), ((), ()))
TN = (((0,), (0,)), ((), ()))


def tile_of(cols, most):
    tile = min(cols, most)
    while cols % tile:
        tile //= 2
    return tile


def pieces(eighths, units):
    starts = [sum(eighths[:i]) * units // 8 for i in range(len(eighths) + 1)]
    return [(a, b - a) for a, b in zip(starts, starts[1:])]


def tile_at(start, cols, most):
    return tile_of(math.gcd(start, cols), most)


def params(mib=48):
    return pltpu.CompilerParams(vmem_limit_bytes=mib * 2**20)


def share(micros):
    return pl.CostEstimate(flops=micros * 10**9, bytes_accessed=0, transcendentals=0)


SHARE = share(30)
TOKEN = jax.ShapeDtypeStruct((8, 128), F32)
TOKEN_SPEC = pl.BlockSpec((8, 128), lambda i: (0, 0))


def flat(block):
    return block.reshape(block.shape[0] * block.shape[1], block.shape[2])


def place_kernel(n, place_ref, hidden_ref, *refs):
    out_refs = refs[-n:]
    cap = out_refs[0].shape[0]
    rows = jnp.dot(place_ref[...], flat(hidden_ref[...]), preferred_element_type=F32)
    rows = rows.astype(BF16)
    for s in range(n):
        out_refs[s][...] = rows[s * cap : (s + 1) * cap]


def place_rows(placing, hidden, n, cols, after=()):
    slots, rows = placing.shape
    tokens, choices, _ = hidden.shape
    cap = slots // n
    tile = tile_of(cols, 1024)
    return pl.pallas_call(
        functools.partial(place_kernel, n),
        grid=(cols // tile,),
        in_specs=[
            pl.BlockSpec((slots, rows), lambda i: (0, 0)),
            pl.BlockSpec((tokens, choices, tile), lambda i: (0, 0, i)),
            *[pl.BlockSpec(memory_space=pl.ANY)] * len(after),
        ],
        out_specs=[pl.BlockSpec((cap, tile), lambda i: (0, i))] * n,
        out_shape=[jax.ShapeDtypeStruct((cap, cols), BF16)] * n,
        compiler_params=params(),
        cost_estimate=share(2),
        name="place",
    )(placing, hidden, *after)


def part_kernel(row_ref, near_ref, far_ref, *refs):
    here_ref, there_ref = refs[-2:]
    slots = here_ref.shape[0]
    half = near_ref.shape[1]
    total = lax.dot_general(
        row_ref[:, :half], near_ref[...], NT, preferred_element_type=F32
    ) + lax.dot_general(row_ref[:, half:], far_ref[...], NT, preferred_element_type=F32)
    here_ref[...] = total[:slots]
    there_ref[...] = total[slots:].astype(BF16)


def partial_product(rows, near, far, start, cols, after=()):
    total, depth = rows.shape
    slots = total // 2
    half = near.shape[1]
    tile = tile_at(start, cols, 512)
    steps, first = cols // tile, start // tile
    weight = pl.BlockSpec((tile, half), lambda i: (first + i, 0))
    return pl.pallas_call(
        part_kernel,
        grid=(steps,),
        in_specs=[
            pl.BlockSpec((total, depth), lambda i: (0, 0)),
            weight,
            weight,
            *[pl.BlockSpec(memory_space=pl.ANY)] * len(after),
        ],
        out_specs=[pl.BlockSpec((slots, tile), lambda i: (0, i))] * 2,
        out_shape=[
            jax.ShapeDtypeStruct((slots, cols), F32),
            jax.ShapeDtypeStruct((slots, cols), BF16),
        ],
        compiler_params=params(),
        cost_estimate=SHARE,
        name="partial_product",
    )(rows, near, far, *after)


def sum_kernel(here_ref, other_ref, *refs):
    out_ref, token_ref = refs[-2:]
    out_ref[...] = (here_ref[...] + other_ref[...].astype(F32)).astype(BF16)
    token_ref[...] = jnp.zeros_like(token_ref)


def sum_of_parts(here, other, before, start, total, after=()):
    slots, cols = here.shape
    tile = tile_at(start, cols, 512)
    steps, first = cols // tile, start // tile
    extra = [*after] if before is None else [before, *after]
    return pl.pallas_call(
        sum_kernel,
        grid=(steps,),
        in_specs=[pl.BlockSpec((slots, tile), lambda i: (0, i))] * 2
        + [pl.BlockSpec(memory_space=pl.ANY)] * len(extra),
        out_specs=[
            pl.BlockSpec((slots, tile), lambda i: (0, first + i)),
            TOKEN_SPEC,
        ],
        out_shape=[jax.ShapeDtypeStruct((slots, total), BF16), TOKEN],
        input_output_aliases={} if before is None else {2: 0},
        compiler_params=params(),
        cost_estimate=SHARE,
        name="sum_of_parts",
    )(here, other, *extra)


def column_piece(blocks, start, cols, after=()):
    count, cap = len(blocks), blocks[0].shape[0]
    tile = tile_at(start, cols, 1024)
    steps, first = cols // tile, start // tile

    def kernel(*refs):
        refs[-1][...] = jnp.concatenate([r[...] for r in refs[:count]], axis=0)

    return pl.pallas_call(
        kernel,
        grid=(steps,),
        in_specs=[pl.BlockSpec((cap, tile), lambda i: (0, first + i))] * count
        + [pl.BlockSpec(memory_space=pl.ANY)] * len(after),
        out_specs=pl.BlockSpec((count * cap, tile), lambda i: (0, i)),
        out_shape=jax.ShapeDtypeStruct((count * cap, cols), BF16),
        compiler_params=params(),
        cost_estimate=SHARE,
        name="column_piece",
    )(*blocks, *after)


def weight_kernel(count, *refs):
    rows_ref, (out_ref, token_ref) = refs[count], refs[-2:]
    token_ref[...] = jnp.zeros_like(token_ref)
    scaled = jnp.concatenate([r[...] for r in refs[:count]], axis=0)
    total = lax.dot_general(scaled, rows_ref[...], TN, preferred_element_type=F32)
    out_ref[...] = total.astype(BF16)


def weight_piece(scaled, row_blocks, before, start, cols, units, after=()):
    count = len(scaled)
    total, width = row_blocks.shape
    tile = functools.reduce(math.gcd, [start - at for _, at in scaled], math.gcd(start, cols))
    tile = tile_of(tile, 512)
    steps, first = cols // tile, start // tile
    extra = [*after] if before is None else [before, *after]

    def block(rows, at):
        skip = (start - at) // tile
        return pl.BlockSpec((rows.shape[0], tile), lambda i: (0, skip + i))

    return pl.pallas_call(
        functools.partial(weight_kernel, count),
        grid=(steps,),
        in_specs=[block(*entry) for entry in scaled]
        + [pl.BlockSpec((total, width), lambda i: (0, 0))]
        + [pl.BlockSpec(memory_space=pl.ANY)] * len(extra),
        out_specs=[
            pl.BlockSpec((tile, width), lambda i: (first + i, 0)),
            TOKEN_SPEC,
        ],
        out_shape=[jax.ShapeDtypeStruct((units, width), BF16), TOKEN],
        input_output_aliases={} if before is None else {count + 1: 0},
        compiler_params=params(),
        cost_estimate=SHARE,
        name="weight_grad",
    )(*[rows for rows, _ in scaled], row_blocks, *extra)


def return_kernel(place_ref, gate_ref, hidden_ref, back_ref, *refs):
    out_ref, part_ref = refs[-2:]
    rows = lax.dot_general(place_ref[...], back_ref[...], TN, preferred_element_type=F32)
    out_ref[...] = (gate_ref[...] * rows).astype(BF16).reshape(out_ref.shape)
    part = jnp.sum(flat(hidden_ref[...]).astype(F32) * rows, axis=1, keepdims=True)

    @pl.when(pl.program_id(0) == 0)
    def _():
        part_ref[...] = part

    @pl.when(pl.program_id(0) > 0)
    def _():
        part_ref[...] += part


def return_rows(onehot, gates, hidden, back, before, start, after=()):
    slots, rows = onehot.shape
    tokens, choices, _ = hidden.shape
    cols = back.shape[1]
    tile = tile_at(start, cols, 1024)
    steps, first = cols // tile, start // tile
    block = pl.BlockSpec((tokens, choices, tile), lambda i: (0, 0, first + i))
    in_specs = [
        pl.BlockSpec((slots, rows), lambda i: (0, 0)),
        pl.BlockSpec((rows, 1), lambda i: (0, 0)),
        block,
        pl.BlockSpec((slots, tile), lambda i: (0, i)),
    ]
    extra = [*after] if before is None else [before, *after]
    return pl.pallas_call(
        return_kernel,
        grid=(steps,),
        in_specs=in_specs + [pl.BlockSpec(memory_space=pl.ANY)] * len(extra),
        out_specs=[block, pl.BlockSpec((rows, 1), lambda i: (0, 0))],
        out_shape=[
            jax.ShapeDtypeStruct(hidden.shape, BF16),
            jax.ShapeDtypeStruct((rows, 1), F32),
        ],
        input_output_aliases={} if before is None else {4: 0},
        compiler_params=params(),
        cost_estimate=SHARE,
        name="return_rows",
    )(onehot, gates, hidden, back, *extra)


def swap(x, axis, bit):
    n = lax.axis_size(axis)
    return lax.ppermute(x, axis, [(i, i ^ bit) for i in range(n)])


def to_experts(rows):
    return lax.all_to_all(rows, "expert", split_axis=0, concat_axis=0, tiled=True)


def chip_features(rows, width):
    dp = lax.axis_index("dp")
    if lax.axis_size("etp") != 2:
        features = lax.all_gather(rows, "etp", axis=1, tiled=True)

        def part(index):
            return lax.dynamic_slice_in_dim(features, index * width, width, axis=1)

        here = jnp.concatenate([part(dp), part(dp ^ 1)], axis=1)
        there = swap(jnp.concatenate([part(dp ^ 2), part(dp ^ 3)], axis=1), "dp", 2)
        return jnp.concatenate([here, there], axis=0)
    first, second = [], []
    for d in range(4):
        for x in range(2):
            if d // 2 == x:
                first.append((d * 2 + x, d * 2 + 1 - x))
            else:
                first.append((d * 2 + x, (d ^ 2) * 2 + x))
                second.append((d * 2 + x, (d ^ 2) * 2 + 1 - x))
    one = lax.ppermute(rows, ("dp", "etp"), first)
    two = lax.ppermute(rows, ("dp", "etp"), second)
    same = dp // 2 == lax.axis_index("etp")
    here, there = jnp.where(same, rows, one), jnp.where(same, one, two)
    both = jnp.concatenate([here, there], axis=0)
    flipped = jnp.concatenate([both[:, width:], both[:, :width]], axis=1)
    return jnp.where(dp % 2 == 0, both, flipped)


def body(out_grad, hidden, gates, expert_ids, down_weight):
    tokens, choices, ff = hidden.shape
    n = lax.axis_size("expert")
    cap = min(tokens, 5 * tokens // (2 * n))
    slots = n * cap
    sums, pieces_of_rows = pieces(SUM_PIECES, ff), pieces(ROW_PIECES, ff)
    early = pieces_of_rows[EARLY][0]
    cut = sums[-1][0]
    width = down_weight.shape[2]
    expert = lax.axis_index("expert")

    near_weight = down_weight[0]
    far_weight = swap(near_weight, "dp", 1)

    flat_ids = expert_ids.reshape(-1)
    member = (flat_ids[:, None] == jnp.arange(n, dtype=jnp.int32)[None, :]).astype(jnp.int32)
    earlier = jnp.cumsum(member, axis=0) - member
    target = flat_ids * cap + jnp.sum(earlier * member, axis=1)
    chosen = target[None, :] == jnp.arange(slots, dtype=jnp.int32)[:, None]
    onehot = chosen.astype(BF16)
    flat_gates = gates.reshape(-1)
    float_gates = flat_gates.astype(F32)[:, None]
    moved = ((flat_ids ^ expert) - flat_ids) * cap + target
    chosen = moved[None, :] == jnp.arange(slots, dtype=jnp.int32)[:, None]
    placing = jnp.where(chosen, flat_gates[None, :], jnp.zeros((), BF16))
    by_token = jnp.sum(chosen.astype(BF16).reshape(slots, tokens, choices), axis=2)

    placed = jnp.dot(by_token, out_grad, preferred_element_type=F32).astype(BF16)
    arrived = [placed[s * cap : (s + 1) * cap] for s in range(n)]
    arrived = [swap(b, "expert", s) if s else b for s, b in enumerate(arrived)]
    grad_rows = jnp.concatenate(arrived, axis=0)
    grad_rows = jnp.concatenate(
        [lax.dynamic_slice_in_dim(grad_rows, (expert ^ e) * cap, cap) for e in range(n)],
        axis=0,
    )

    [own] = place_rows(placing[:cap], hidden, 1, early, (placed,))
    own_across = swap(own, "dp", 2)
    blocks = place_rows(placing, hidden, n, ff, (own,))
    grad_rows, far_weight, _, *blocks = lax.optimization_barrier(
        (grad_rows, far_weight, own_across, *blocks)
    )
    scaled = [swap(b, "expert", s) if s else b for s, b in enumerate(blocks)]
    rows = chip_features(grad_rows, width)

    here, others, near, across, traded = [], [], [], [], []
    hidden_grad, weight_grad = None, None
    gate_parts = []

    def part(j, after):
        h, t = partial_product(rows, near_weight, far_weight, *sums[j], after)
        here.append(h)
        others.append(swap(t, "dp", 2))
        return t

    def send(j, after):
        near.append(column_piece(scaled[1:] if j < EARLY else scaled, *pieces_of_rows[j], after))
        across.append(swap(near[j], "dp", 2))
        return near[j]

    def trade(j, after):
        *parts, _ = lax.optimization_barrier((near[j], across[j], after))
        traded.append([swap(p, "dp", 1) for p in parts])

    def weight(j, after, skip=0, take=16):
        at, cols = pieces_of_rows[j]
        parts = [(p, at) for p in (near[j], across[j], *traded[j])]
        if j < EARLY:
            parts = [p for own, part in zip(own_parts, parts) for p in ((own, 0), part)]
        skip, take = skip * ff // 16, take * ff // 16
        start, cols = at + skip, min(cols - skip, take)
        return weight_piece(parts, row_blocks, weight_grad, start, cols, ff, (after,))

    def give_back(back, start, after):
        out, part = return_rows(
            onehot, float_gates, hidden, back, hidden_grad, start, (after,)
        )
        gate_parts.append(part)
        return out

    token = part(0, ())
    token = part(1, (token,))
    token = part(2, (token, others[0]))
    first, token = sum_of_parts(here[0], others[0], None, sums[0][0], cut, (token,))
    token = part(3, (token, others[1]))
    first, token = sum_of_parts(here[1], others[1], first, sums[1][0], cut, (token,))
    first, token = sum_of_parts(here[2], others[2], first, sums[2][0], cut, (token,))
    first_back = to_experts(first)
    token = send(0, (token,))
    far_rows, _ = lax.optimization_barrier((rows[:, width:], token))
    far_rows = swap(far_rows, "dp", 1)
    second, token = sum_of_parts(here[3], others[3], None, 0, ff - cut, (token,))
    far_rows, _ = lax.optimization_barrier((far_rows, token))
    row_blocks = jnp.concatenate([rows[:, :width], far_rows], axis=0)
    row_blocks = row_blocks.reshape(4, n, cap, width)
    row_blocks = jnp.concatenate(
        [lax.dynamic_slice_in_dim(row_blocks, expert ^ s, 1, axis=1) for s in range(n)],
        axis=1,
    ).reshape(4 * slots, width)
    token = send(1, (token, row_blocks))
    *moving, _ = lax.optimization_barrier((own, own_across, token))
    own_parts = [own, own_across, *[swap(p, "dp", 1) for p in moving]]
    token = send(2, (token,))
    trade(0, token)
    token = send(3, (token, *own_parts))
    weight_grad, token = weight(0, token, 0, 2)
    second, _, _ = lax.optimization_barrier((second, first_back, token))
    second_back = to_experts(second)
    hidden_grad = give_back(first_back, 0, token)
    trade(1, gate_parts[0])
    weight_grad, token = weight(0, gate_parts[0], 2)
    token = send(4, (token,))
    most = 5 if ff % 2048 == 0 else 4
    weight_grad, token = weight(1, token, 0, most)
    trade(2, token)
    weight_grad, token = weight(1, token, most)
    trade(3, token)
    weight_grad, token = weight(2, token)
    weight_grad, token = weight(3, token)
    trade(4, token)
    hidden_grad = give_back(second_back, cut, token)
    weight_grad, token = weight(4, gate_parts[1])
    gate_total = sum(gate_parts)
    if lax.axis_size("etp") == 2:
        gate_total = gate_total + swap(gate_total, "etp", 1) + token[:1, :1]
    else:
        gate_total = lax.psum(gate_total, "etp")

    return (
        hidden_grad,
        gate_total.astype(BF16).reshape(gates.shape),
        weight_grad[None],
    )


def solution(mesh):
    return jax.shard_map(
        body,
        mesh=mesh,
        in_specs=(
            P(("dp", "expert"), "etp"),
            P(("dp", "expert"), None, "etp"),
            P(("dp", "expert"), None),
            P(("dp", "expert"), None),
            P("expert", "etp", "dp"),
        ),
        out_specs=(
            P(("dp", "expert"), None, "etp"),
            P(("dp", "expert"), None),
            P("expert", "etp", "dp"),
        ),
        check_vma=False,
    )
```
